256 devices in a mesh: gx: 4 (over x_hi, core), gy: 8 (over z), gz: 8 (over y, x_lo).
Axes of the slice: x: 4 (x_hi: 2, x_lo: 2; x = x_hi * 2 + x_lo), y: 4, z: 8, core: 2. Of those that a mesh axis runs over, the one named last changes fastest.
Arguments:
- sdf: float32 [64, 512, 1024], P('gx', 'gy', 'gz'), may hold values from -6 to 6
- albedo: float32 [64, 512, 1024], P('gx', 'gy', 'gz'), may hold values from 0.25 to 1
- intensity: float32 [64, 512, 1024], P('gx', 'gy', 'gz'), may hold values from -6 to 6
- direction: float32 [64, 512, 1024], P('gx', 'gy', 'gz'), may hold values from -6 to 6
- lighting: float32 [9], replicated, may hold values from -4 to 4
Outputs:
- gradient: float32 [64, 512, 1024], P('gx', 'gy', 'gz')
- hess_vec: float32 [64, 512, 1024], P('gx', 'gy', 'gz')
- light_grad: float32 [9], replicated
The draws below stay inside these ranges and needn't reach their ends.
All inputs are finite; a program needn't handle non-finite values.
Results may differ from the reference program's by a relative error of at most 0.00015.
Values sent between devices are 32-bit elements; how exact they have to be, the bound alone decides.
No kernel may reach another device: no remote copies, remote signals or barrier semaphores. Data moves between devices by JAX's collectives and lax.ppermute only.
A program may use at most 128 MiB of HBM per device.

```python
import math
import jax
import jax.numpy as jnp

NX = 64
NY = 512
NZ = 1024


def steps_of(key, shape, shards, low, high):
    level, own = 1.0, jax.random.fold_in(key, 6)
    for position, shards_of in shards:
        draws = jnp.exp(jax.random.uniform(jax.random.fold_in(own, position), (shards_of,), jnp.float32, low / len(shards), high / len(shards)))
        level = level * jnp.repeat(draws, shape[position] // shards_of).reshape([-1 if axis == position else 1 for axis in range(len(shape))])
    return level


def centred(key, dims, spread, limit, shards=(), dtype=jnp.bfloat16):
    array = jax.random.normal(key, dims, jnp.float32) * spread
    if len(shards) > 0:
        array = steps_of(key, dims, shards, -0.22, 0.18) * array
    return jnp.clip(array, min=-limit, max=limit).astype(dtype)


def setup_inputs(seed: int = 0) -> dict:
    seeds = jax.random.split(jax.random.key(seed), 6)
    sdf = centred(seeds[0], (NX, NY, NZ), 1.0, 6.0, ((0, 4), (1, 8), (2, 8)), jnp.float32)
    albedo = jnp.clip(jnp.exp(math.log(1.0) - 1.3862944 * jax.random.uniform(seeds[1], (NX, NY, NZ), jnp.float32) ** steps_of(seeds[1], (NX, NY, NZ), ((0, 4), (1, 8), (2, 8)), -0.2, 0.2)), 0.25, 1.0)
    intensity = centred(seeds[2], (NX, NY, NZ), 1.0, 6.0, ((0, 4), (1, 8), (2, 8)), jnp.float32)
    direction = centred(seeds[3], (NX, NY, NZ), 1.0, 6.0, ((0, 4), (1, 8), (2, 8)), jnp.float32)
    lighting = centred(seeds[4], (9,), 1.0, 4.0, (), jnp.float32)
    return dict(sdf=sdf, albedo=albedo, intensity=intensity, direction=direction, lighting=lighting)


soften = 0.25
reg_weight = 0.02
sh_zero = 0.282095
sh_one = 0.488603
sh_two = 1.092548
sh_three = 0.315392
sh_four = 0.546274

def central(field):
    return ((field[..., 2:, 1:-1, 1:-1] - field[..., :-2, 1:-1, 1:-1]) * 0.5, (field[..., 1:-1, 2:, 1:-1] - field[..., 1:-1, :-2, 1:-1]) * 0.5, (field[..., 1:-1, 1:-1, 2:] - field[..., 1:-1, 1:-1, :-2]) * 0.5)

def laplace(field):
    return field[..., 2:, 1:-1, 1:-1] + field[..., :-2, 1:-1, 1:-1] + field[..., 1:-1, 2:, 1:-1] + field[..., 1:-1, :-2, 1:-1] + field[..., 1:-1, 1:-1, 2:] + field[..., 1:-1, 1:-1, :-2] - 6.0 * field[..., 1:-1, 1:-1, 1:-1]

def diverge(fx, fy, fz):
    return (fx[..., 2:, 1:-1, 1:-1] - fx[..., :-2, 1:-1, 1:-1] + (fy[..., 1:-1, 2:, 1:-1] - fy[..., 1:-1, :-2, 1:-1]) + (fz[..., 1:-1, 1:-1, 2:] - fz[..., 1:-1, 1:-1, :-2])) * 0.5

def shading(grads, lighting, albedo, intensity):
    scale = jnp.sqrt(grads[0] * grads[0] + grads[1] * grads[1] + grads[2] * grads[2] + soften)
    nrm_x = grads[0] / scale
    nrm_y = grads[1] / scale
    nrm_z = grads[2] / scale
    basis = [jnp.full_like(nrm_x, sh_zero), sh_one * nrm_y, sh_one * nrm_z, sh_one * nrm_x, sh_two * nrm_x * nrm_y, sh_two * nrm_y * nrm_z, sh_three * (3.0 * nrm_z * nrm_z - 1.0), sh_two * nrm_x * nrm_z, sh_four * (nrm_x * nrm_x - nrm_y * nrm_y)]
    shade = basis[0] * lighting[0]
    for index in range(1, 9):
        shade = shade + lighting[index] * basis[index]
    res = albedo * shade - intensity
    l_vals = lighting
    part_x = sh_one * l_vals[3] + sh_two * (l_vals[4] * nrm_y + l_vals[7] * nrm_z) + 2.0 * sh_four * l_vals[8] * nrm_x
    part_y = sh_one * l_vals[1] + sh_two * (l_vals[4] * nrm_x + l_vals[5] * nrm_z) - 2.0 * sh_four * l_vals[8] * nrm_y
    part_z = sh_one * l_vals[2] + sh_two * (l_vals[5] * nrm_y + l_vals[7] * nrm_x) + 6.0 * sh_three * l_vals[6] * nrm_z
    along = nrm_x * part_x + nrm_y * part_y + nrm_z * part_z
    factor = albedo / scale
    jac = ((part_x - nrm_x * along) * factor, (part_y - nrm_y * along) * factor, (part_z - nrm_z * along) * factor)
    return (res, jac, basis)

def reference(sdf, albedo, intensity, direction, lighting):
    padded_d = jnp.pad(sdf, 1)
    padded_v = jnp.pad(direction, 1)
    res, jac, basis = shading(central(padded_d), lighting, albedo, intensity)
    grad_v = central(padded_v)
    lin = jac[0] * grad_v[0] + jac[1] * grad_v[1] + jac[2] * grad_v[2]
    lap_d = laplace(padded_d)
    lap_v = laplace(padded_v)
    energy = 0.5 * jnp.sum(res * res) + 0.5 * reg_weight * jnp.sum(lap_d * lap_d)
    light_grad = jnp.stack([jnp.sum(albedo * term * res) for term in basis])
    damping = energy / (NX * NY * NZ)
    gradient = -diverge(jnp.pad(res * jac[0], 1), jnp.pad(res * jac[1], 1), jnp.pad(res * jac[2], 1)) + reg_weight * laplace(jnp.pad(lap_d, 1))
    hess_vec = -diverge(jnp.pad(lin * jac[0], 1), jnp.pad(lin * jac[1], 1), jnp.pad(lin * jac[2], 1)) + reg_weight * laplace(jnp.pad(lap_v, 1)) + damping * direction
    return (gradient, hess_vec, light_grad)
```

```python
import jax
import jax.numpy as jnp
from jax import lax
from jax.experimental import pallas as pl
from jax.experimental.pallas import tpu as pltpu
from jax.sharding import PartitionSpec as P

reg_weight = 0.02
sh_zero = 0.282095
sh_one = 0.488603
sh_two = 1.092548
sh_three = 0.315392
sh_four = 0.546274

AXES = ("gx", "gy", "gz")
LANES = 128
ROWS = 8
PAD = 8
PARAMS = pltpu.CompilerParams(vmem_limit_bytes=40 * 1024 * 1024)


def lane_ids(rows):
    return lax.broadcasted_iota(jnp.int32, (rows, LANES), 1)


def fold(tall, width):
    parts = LANES // width
    rows = tall.shape[0] // parts
    lanes = lane_ids(rows)
    out = tall[:rows]
    for g in range(1, parts):
        moved = pltpu.roll(tall[g * rows : (g + 1) * rows], g * width, 1)
        out = jnp.where((lanes >= g * width) & (lanes < (g + 1) * width), moved, out)
    return out


def unfold(packed, width):
    parts = LANES // width
    pieces = [packed] + [pltpu.roll(packed, LANES - g * width, 1) for g in range(1, parts)]
    return jnp.concatenate(pieces, axis=0)


def edge_flags():
    flags = []
    for axis in AXES:
        index, count = lax.axis_index(axis), lax.axis_size(axis)
        flags.append(
            (
                jnp.where(index > 0, 1.0, 0.0).astype(jnp.float32),
                jnp.where(index < count - 1, 1.0, 0.0).astype(jnp.float32),
            )
        )
    return flags


def pack_kernel(d_ref, v_ref, xu, xd, yu, yd, zu, zd):
    nx, ny, nz = d_ref.shape
    lanes = lane_ids(ny)
    up = jnp.zeros((ny, LANES), jnp.float32)
    down = jnp.zeros((ny, LANES), jnp.float32)
    for f, ref in enumerate((d_ref, v_ref)):
        xu[f] = ref[nx - 1]
        xd[f] = ref[0]
        for x in range(nx):
            yu[f, x : x + 1, :] = ref[x, ny - 1 : ny, :]
            yd[f, x : x + 1, :] = ref[x, 0:1, :]
            lane = f * nx + x
            plane = ref[x]
            up = jnp.where(lanes == lane, pltpu.roll(plane, lane + 1, 1), up)
            moved = plane if lane == 0 else pltpu.roll(plane, lane, 1)
            down = jnp.where(lanes == lane, moved, down)
    zu[...] = fold(up, 2 * nx)
    zd[...] = fold(down, 2 * nx)


def main_kernel(
    light, d_ref, a_ref, i_ref, v_ref, xp, xn, yp, yn, zp, zn,
    gp, hp, mxu, mxd, myu, myd, mzu, mzd, sums,
    dpad, vpad, zprev, znext, cent, ay, by, bx, ax, zup, zdn, accs,
):
    nx, ny, nz = d_ref.shape
    (fxp, fxn), (fyp, fyn), (fzp, fzn) = edge_flags()
    for f, (ref, pad) in enumerate(((d_ref, dpad), (v_ref, vpad))):
        pad[1 : nx + 1, PAD : PAD + ny, :] = ref[...]
        pad[0, PAD : PAD + ny, :] = xp[f] * fxp
        pad[nx + 1, PAD : PAD + ny, :] = xn[f] * fxn
        before = yp[f] * fyp
        after = yn[f] * fyn
        for x in range(nx):
            pad[x + 1, PAD - 1 : PAD, :] = before[x : x + 1]
            pad[x + 1, PAD + ny : PAD + ny + 1, :] = after[x : x + 1]
    zprev[...] = unfold(zp[...] * fzp, 2 * nx)
    znext[...] = unfold(zn[...] * fzn, 2 * nx)
    zero_row = jnp.zeros((1, LANES), jnp.float32)
    for u in range(2):
        ay[u, PAD + ny : PAD + ny + 1, :] = zero_row
        by[u, PAD - 1 : PAD, :] = zero_row
    zero = jnp.zeros((ROWS, LANES), jnp.float32)
    zup[...] = jnp.zeros((ny, LANES), jnp.float32)
    zdn[...] = jnp.zeros((ny, LANES), jnp.float32)
    bx[...] = jnp.zeros(bx.shape, jnp.float32)
    gp[0] = jnp.zeros((ny, LANES), jnp.float32)
    hp[0] = jnp.zeros((ny, LANES), jnp.float32)
    for k in range(accs.shape[0]):
        accs[k] = zero

    l = [light[k] for k in range(9)]
    c1, c2, c3 = sh_one * l[1], sh_one * l[2], sh_one * l[3]
    c4, c5, c7 = sh_two * l[4], sh_two * l[5], sh_two * l[7]
    c6, c8 = 6.0 * sh_three * l[6], 2.0 * sh_four * l[8]
    base = sh_zero * l[0] - sh_three * l[6]
    lanes = lane_ids(ROWS)
    first, final = lanes == 0, lanes == LANES - 1

    def shifted(pad, f, x, at, mid):
        xm = pad[x, at : at + ROWS, :]
        xq = pad[x + 2, at : at + ROWS, :]
        ym = pad[x + 1, at - 1 : at - 1 + ROWS, :]
        yq = pad[x + 1, at + 1 : at + 1 + ROWS, :]
        lane = f * nx + x
        rows = slice(at - PAD, at - PAD + ROWS)
        halo_m = pltpu.roll(zprev[rows, :], (LANES - lane) & (LANES - 1), 1)
        halo_q = pltpu.roll(znext[rows, :], LANES - 1 - lane, 1)
        zm = jnp.where(first, halo_m, pltpu.roll(mid, 1, 1))
        zq = jnp.where(final, halo_q, pltpu.roll(mid, LANES - 1, 1))
        lap = (xm + xq) + (ym + yq) + (zm + zq) - 6.0 * mid
        return xq - xm, yq - ym, zq - zm, lap

    def plane(x, _):
        for c in range(ny // ROWS):
            at = PAD + c * ROWS
            rows = slice(c * ROWS, (c + 1) * ROWS)
            mid = dpad[x + 1, at : at + ROWS, :]
            hx, hy, hz, lap = shifted(dpad, 0, x, at, mid)
            inv = lax.rsqrt(hx * hx + hy * hy + hz * hz + 1.0)
            nrx, nry, nrz = hx * inv, hy * inv, hz * inv
            px = c3 + c4 * nry + c7 * nrz + c8 * nrx
            py = c1 + c4 * nrx + c5 * nrz - c8 * nry
            pz = c2 + c5 * nry + c7 * nrx + c6 * nrz
            along = nrx * px + nry * py + nrz * pz
            linear = c1 * nry + c2 * nrz + c3 * nrx
            shade = base + 0.5 * (along + linear)
            albedo = a_ref[x, rows, :]
            res = albedo * shade - i_ref[x, rows, :]
            qx, qy, qz = px - nrx * along, py - nry * along, pz - nrz * along
            scale = albedo * inv
            w = albedo * res
            wx, wy, wz = w * nrx, w * nry, w * nrz
            terms = (
                w, wy, wz, wx, wx * nry, wy * nrz, wz * nrz, wx * nrz,
                wx * nrx - wy * nry, res * res + reg_weight * (lap * lap),
            )
            for k, term in enumerate(terms):
                accs[k] = accs[k] + term
            vmid = vpad[x + 1, at : at + ROWS, :]
            ux, uy, uz, vlap = shifted(vpad, 1, x, at, vmid)
            lin = scale * (qx * ux + qy * uy + qz * uz)
            for u, (weight, lapl) in enumerate(((res * scale, lap), (lin * scale, vlap))):
                reg = reg_weight * lapl
                rx, ry, rz = weight * qx, weight * qy, weight * qz
                ay[u, at : at + ROWS, :] = reg - ry
                by[u, at : at + ROWS, :] = reg + ry
                lane = u * nx + x
                fwd = pltpu.roll(reg + rz, 1, 1)
                bwd = pltpu.roll(reg - rz, LANES - 1, 1)
                zup[rows, :] = jnp.where(lanes == lane, pltpu.roll(fwd, lane, 1), zup[rows, :])
                zdn[rows, :] = jnp.where(lanes == lane, pltpu.roll(bwd, lane + 1, 1), zdn[rows, :])
                out = (gp, hp)[u]
                out[x, rows, :] = out[x, rows, :] + (reg - rx)
                cent[u, rows, :] = (
                    bx[u, rows, :]
                    - 6.0 * reg
                    + jnp.where(first, 0.0, fwd)
                    + jnp.where(final, 0.0, bwd)
                )
                bx[u, rows, :] = reg + rx
        for u in range(2):
            out = (gp, hp)[u]
            for c in range(ny // ROWS):
                at = PAD + c * ROWS
                rows = slice(c * ROWS, (c + 1) * ROWS)
                out[x + 1, rows, :] = (
                    cent[u, rows, :]
                    + ay[u, at + 1 : at + 1 + ROWS, :]
                    + by[u, at - 1 : at - 1 + ROWS, :]
                )
            myd[u, pl.ds(x, 1), :] = ay[u, PAD : PAD + 1, :]
            myu[u, pl.ds(x, 1), :] = by[u, PAD + ny - 1 : PAD + ny, :]
        return 0

    lax.fori_loop(0, nx, plane, 0)
    for u in range(2):
        mxu[u] = bx[u]
        mxd[u] = (gp, hp)[u][0]
    mzu[...] = fold(zup[...], 2 * nx)
    mzd[...] = fold(zdn[...], 2 * nx)
    line = lax.broadcasted_iota(jnp.int32, (1, LANES), 1)
    row = jnp.zeros((1, LANES), jnp.float32)
    for k in range(accs.shape[0]):
        row = jnp.where(line == k, jnp.sum(accs[k]), row)
    sums[...] = jnp.broadcast_to(row, sums.shape)


def final_kernel(count, all_sums, v_ref, gp, hp, xp, xn, yp, yn, zp, zn, g_ref, h_ref, t_ref, zprev, znext):
    nx, ny, nz = v_ref.shape
    (fxp, fxn), (fyp, fyn), (fzp, fzn) = edge_flags()
    row = jnp.sum(all_sums[...], axis=0, keepdims=True)
    line = lax.broadcasted_iota(jnp.int32, (1, LANES), 1)
    damping = jnp.sum(jnp.where(line == 9, row, 0.0)) * (0.5 / count)
    weight = jnp.where(line == 0, sh_zero, 0.0)
    for k, factor in enumerate((sh_one, sh_one, sh_one, sh_two, sh_two, 3.0 * sh_three, sh_two, sh_four)):
        weight = jnp.where(line == k + 1, factor, weight)
    shift = jnp.sum(jnp.where(line == 0, row, 0.0)) * sh_three
    t_ref[...] = row * weight - jnp.where(line == 6, shift, 0.0)
    zprev[...] = unfold(zp[...] * fzp, 2 * nx)
    znext[...] = unfold(zn[...] * fzn, 2 * nx)
    lanes = lane_ids(ny)
    first, final = lanes == 0, lanes == LANES - 1
    for u, (ref, out) in enumerate(((gp, g_ref), (hp, h_ref))):
        before = yp[u] * fyp
        after = yn[u] * fyn
        for x in range(nx):
            lane = u * nx + x
            value = ref[x + 1]
            value = value + jnp.where(first, pltpu.roll(zprev[...], (LANES - lane) % LANES, 1), 0.0)
            value = value + jnp.where(final, pltpu.roll(znext[...], LANES - 1 - lane, 1), 0.0)
            if u == 1:
                value = value + damping * v_ref[x]
            if x == 0:
                value = value + xp[u] * fxp
            if x == nx - 1:
                value = value + xn[u] * fxn
            out[x] = value
            out[x, 0:1, :] = out[x, 0:1, :] + before[x : x + 1]
            out[x, ny - 1 : ny, :] = out[x, ny - 1 : ny, :] + after[x : x + 1]


def exchange(ups, downs):
    got = []
    for axis, up, down in zip(AXES, ups, downs):
        count = lax.axis_size(axis)
        forward = [(i, (i + 1) % count) for i in range(count)]
        backward = [(j, i) for i, j in forward]
        got.append(lax.ppermute(up, axis, forward))
        got.append(lax.ppermute(down, axis, backward))
    return got


def body(sdf, albedo, intensity, direction, lighting):
    nx, ny, nz = sdf.shape
    devices = 1
    for axis in AXES:
        devices *= lax.axis_size(axis)
    count = float(nx * ny * nz) * devices
    f32 = lambda *shape: jax.ShapeDtypeStruct(shape, jnp.float32)
    rows = ny * 2 * nx // LANES
    faces = [f32(2, ny, nz)] * 2 + [f32(2, nx, nz)] * 2 + [f32(rows, LANES)] * 2
    vmem = pl.BlockSpec(memory_space=pltpu.VMEM)
    smem = pl.BlockSpec(memory_space=pltpu.SMEM)

    xu, xd, yu, yd, zu, zd = pl.pallas_call(
        pack_kernel, out_shape=faces, in_specs=[vmem] * 2, out_specs=[vmem] * 6, compiler_params=PARAMS
    )(sdf, direction)
    halos = exchange((xu, yu, zu), (xd, yd, zd))
    scratch = lambda *shape: pltpu.VMEM(shape, jnp.float32)
    tall = ny + 2 * PAD
    gp, hp, xu, xd, yu, yd, zu, zd, sums = pl.pallas_call(
        main_kernel,
        out_shape=[f32(nx + 1, ny, nz)] * 2 + faces + [f32(devices, LANES)],
        in_specs=[smem] + [vmem] * 10,
        out_specs=[vmem] * 9,
        scratch_shapes=[
            scratch(nx + 2, tall, nz), scratch(nx + 2, tall, nz),
            scratch(ny, LANES), scratch(ny, LANES),
            scratch(2, ny, nz), scratch(2, tall, nz), scratch(2, tall, nz),
            scratch(2, ny, nz), scratch(2, ny, nz),
            scratch(ny, LANES), scratch(ny, LANES), scratch(10, ROWS, LANES),
        ],
        compiler_params=PARAMS,
    )(lighting, sdf, albedo, intensity, direction, *halos)
    halos = exchange((xu, yu, zu), (xd, yd, zd))
    all_sums = lax.all_to_all(sums, AXES, 0, 0, tiled=True)
    gradient, hess_vec, totals = pl.pallas_call(
        lambda *refs: final_kernel(count, *refs),
        out_shape=[f32(nx, ny, nz)] * 2 + [f32(1, LANES)],
        in_specs=[vmem] * 10,
        out_specs=[vmem] * 3,
        scratch_shapes=[scratch(ny, LANES), scratch(ny, LANES)],
        compiler_params=PARAMS,
    )(all_sums, direction, gp, hp, *halos)
    return gradient, hess_vec, totals[0, :9]


def solution(mesh):
    grid = P("gx", "gy", "gz")
    return jax.shard_map(
        body,
        mesh=mesh,
        in_specs=(grid, grid, grid, grid, P()),
        out_specs=(grid, grid, P()),
        check_vma=False,
    )
```

```python
import jax
import jax.numpy as jnp
from jax import lax
from jax.experimental import pallas as pl
from jax.experimental.pallas import tpu as pltpu
from jax.sharding import PartitionSpec as P

reg_weight = 0.02
sh_zero = 0.282095
sh_one = 0.488603
sh_two = 1.092548
sh_three = 0.315392
sh_four = 0.546274

AXES = ("gx", "gy", "gz")
LANES = 128
ROWS = 8
PAD = 8
PARAMS = pltpu.CompilerParams(vmem_limit_bytes=40 * 1024 * 1024)


def lane_ids(rows):
    return lax.broadcasted_iota(jnp.int32, (rows, LANES), 1)


def fold(tall, width):
    parts = LANES // width
    rows = tall.shape[0] // parts
    lanes = lane_ids(rows)
    out = tall[:rows]
    for g in range(1, parts):
        moved = pltpu.roll(tall[g * rows : (g + 1) * rows], g * width, 1)
        out = jnp.where((lanes >= g * width) & (lanes < (g + 1) * width), moved, out)
    return out


def unfold(packed, width):
    parts = LANES // width
    pieces = [packed] + [pltpu.roll(packed, LANES - g * width, 1) for g in range(1, parts)]
    return jnp.concatenate(pieces, axis=0)


def edge_flags():
    flags = []
    for axis in AXES:
        index, count = lax.axis_index(axis), lax.axis_size(axis)
        flags.append(
            (
                lax.rem(index, 2) == 0,
                jnp.where(index > 0, 1.0, 0.0).astype(jnp.float32),
                jnp.where(index < count - 1, 1.0, 0.0).astype(jnp.float32),
            )
        )
    return flags


def sides(flag, first, second):
    even, before, after = flag
    return jnp.where(even, second, first) * before, jnp.where(even, first, second) * after


def both_sides(flag, first, second, width):
    before, after = sides(flag, first, second)
    odd = lax.rem(lane_ids(first.shape[0]), 2) == 1
    return unfold(jnp.where(odd, before, after), width)


def pack_kernel(d_hbm, v_hbm, x1, x2, y1, y2, zm, d_ref, v_ref, sems):
    nx, ny, nz = d_ref.shape
    half = nx // 2
    copies = []
    for f, (src, dst) in enumerate(((d_hbm, d_ref), (v_hbm, v_ref))):
        for h in range(2):
            part = pl.ds(h * half, half)
            copy = pltpu.make_async_copy(src.at[part], dst.at[part], sems.at[f, h])
            copy.start()
            copies.append(copy)
    (xe, _, _), (ye, _, _), _ = edge_flags()
    lanes = lane_ids(ny)
    edge = lanes == 0
    pair = lanes // 2
    packed = jnp.zeros((ny, LANES), jnp.float32)
    for f, ref in enumerate((d_ref, v_ref)):
        for h in range(2):
            copies[2 * f + h].wait()
            for x in range(h * half, (h + 1) * half):
                top, bottom = ref[x, ny - 1 : ny, :], ref[x, 0:1, :]
                y1[f, x : x + 1, :] = jnp.where(ye, top, bottom)
                y2[f, x : x + 1, :] = jnp.where(ye, bottom, top)
                plane = ref[x]
                slot = f * nx + x
                up = pltpu.roll(plane, (2 * slot + 2) % LANES, 1)
                down = pltpu.roll(plane, 2 * slot, 1) if slot else plane
                odd = lanes == 2 * slot + 1
                packed = jnp.where(odd, up, jnp.where(lanes == 2 * slot, down, packed))
        x1[f] = jnp.where(xe, ref[nx - 1], ref[0])
        x2[f] = jnp.where(xe, ref[0], ref[nx - 1])
    zm[...] = fold(packed, 4 * nx)


def main_kernel(
    light, d_ref, a_ref, i_ref, v_ref, x1, x2, y1, y2, z1, z2,
    gp, hp, mx1, mx2, my1, my2, mz, sums,
    dpad, vpad, halo, cent, ay, by, bx, zm, myu, myd, accs,
):
    nx, ny, nz = d_ref.shape
    fx, fy, fz = edge_flags()
    for f, (ref, pad) in enumerate(((d_ref, dpad), (v_ref, vpad))):
        pad[1 : nx + 1, PAD : PAD + ny, :] = ref[...]
        before, after = sides(fx, x1[f], x2[f])
        pad[0, PAD : PAD + ny, :] = before
        pad[nx + 1, PAD : PAD + ny, :] = after
        before, after = sides(fy, y1[f], y2[f])
        for x in range(nx):
            pad[x + 1, PAD - 1 : PAD, :] = before[x : x + 1]
            pad[x + 1, PAD + ny : PAD + ny + 1, :] = after[x : x + 1]
    halo[...] = both_sides(fz, z1[...], z2[...], 4 * nx)
    zero_row = jnp.zeros((1, LANES), jnp.float32)
    for u in range(2):
        ay[u, PAD + ny : PAD + ny + 1, :] = zero_row
        by[u, PAD - 1 : PAD, :] = zero_row
    zero = jnp.zeros((ROWS, LANES), jnp.float32)
    zm[...] = jnp.zeros((ny, LANES), jnp.float32)
    bx[...] = jnp.zeros(bx.shape, jnp.float32)
    gp[0] = jnp.zeros((ny, LANES), jnp.float32)
    hp[0] = jnp.zeros((ny, LANES), jnp.float32)
    for k in range(accs.shape[0]):
        accs[k] = zero

    l = [light[k] for k in range(9)]
    c1, c2, c3 = sh_one * l[1], sh_one * l[2], sh_one * l[3]
    c4, c5, c7 = sh_two * l[4], sh_two * l[5], sh_two * l[7]
    c6, c8 = 6.0 * sh_three * l[6], 2.0 * sh_four * l[8]
    base = sh_zero * l[0] - sh_three * l[6]
    lanes = lane_ids(ROWS)
    first, final, pair = lanes == 0, lanes == LANES - 1, lanes // 2

    def shifted(pad, f, x, at, mid):
        xm = pad[x, at : at + ROWS, :]
        xq = pad[x + 2, at : at + ROWS, :]
        ym = pad[x + 1, at - 1 : at - 1 + ROWS, :]
        yq = pad[x + 1, at + 1 : at + 1 + ROWS, :]
        lane = f * nx + x
        rows = slice(at - PAD, at - PAD + ROWS)
        edges = pltpu.roll(halo[rows, :], LANES - 1 - 2 * lane, 1)
        below = jnp.where(first, edges, pltpu.roll(mid, 1, 1))
        above = jnp.where(final, edges, pltpu.roll(mid, LANES - 1, 1))
        lap = (xm + xq) + (ym + yq) + (below + above) - 6.0 * mid
        return xq - xm, yq - ym, above - below, lap

    def plane(x, _):
        for c in range(ny // ROWS):
            at = PAD + c * ROWS
            rows = slice(c * ROWS, (c + 1) * ROWS)
            mid = dpad[x + 1, at : at + ROWS, :]
            hx, hy, hz, lap = shifted(dpad, 0, x, at, mid)
            inv = lax.rsqrt(hx * hx + hy * hy + hz * hz + 1.0)
            nrx, nry, nrz = hx * inv, hy * inv, hz * inv
            px = c3 + c4 * nry + c7 * nrz + c8 * nrx
            py = c1 + c4 * nrx + c5 * nrz - c8 * nry
            pz = c2 + c5 * nry + c7 * nrx + c6 * nrz
            along = nrx * px + nry * py + nrz * pz
            linear = c1 * nry + c2 * nrz + c3 * nrx
            shade = base + 0.5 * (along + linear)
            albedo = a_ref[x, rows, :]
            res = albedo * shade - i_ref[x, rows, :]
            qx, qy, qz = px - nrx * along, py - nry * along, pz - nrz * along
            scale = albedo * inv
            w = albedo * res
            wx, wy, wz = w * nrx, w * nry, w * nrz
            terms = (
                w, wy, wz, wx, wx * nry, wy * nrz, wz * nrz, wx * nrz,
                wx * nrx - wy * nry, res * res + reg_weight * (lap * lap),
            )
            for k, term in enumerate(terms):
                accs[k] = accs[k] + term
            vmid = vpad[x + 1, at : at + ROWS, :]
            ux, uy, uz, vlap = shifted(vpad, 1, x, at, vmid)
            lin = scale * (qx * ux + qy * uy + qz * uz)
            for u, (weight, lapl) in enumerate(((res * scale, lap), (lin * scale, vlap))):
                reg = reg_weight * lapl
                rx, ry, rz = weight * qx, weight * qy, weight * qz
                ay[u, at : at + ROWS, :] = reg - ry
                by[u, at : at + ROWS, :] = reg + ry
                lane = u * nx + x
                fwd = pltpu.roll(reg + rz, 1, 1)
                bwd = pltpu.roll(reg - rz, LANES - 1, 1)
                edges = pltpu.roll(jnp.where(first, fwd, bwd), 2 * lane + 1, 1)
                zm[rows, :] = jnp.where(pair == lane, edges, zm[rows, :])
                out = (gp, hp)[u]
                out[x, rows, :] = out[x, rows, :] + (reg - rx)
                cent[u, rows, :] = (
                    bx[u, rows, :]
                    - 6.0 * reg
                    + jnp.where(first, 0.0, fwd)
                    + jnp.where(final, 0.0, bwd)
                )
                bx[u, rows, :] = reg + rx
        for u in range(2):
            out = (gp, hp)[u]
            for c in range(ny // ROWS):
                at = PAD + c * ROWS
                rows = slice(c * ROWS, (c + 1) * ROWS)
                out[x + 1, rows, :] = (
                    cent[u, rows, :]
                    + ay[u, at + 1 : at + 1 + ROWS, :]
                    + by[u, at - 1 : at - 1 + ROWS, :]
                )
            myd[u, pl.ds(x, 1), :] = ay[u, PAD : PAD + 1, :]
            myu[u, pl.ds(x, 1), :] = by[u, PAD + ny - 1 : PAD + ny, :]
        return 0

    lax.fori_loop(0, nx, plane, 0)
    for u in range(2):
        low = (gp, hp)[u][0]
        mx1[u] = jnp.where(fx[0], bx[u], low)
        mx2[u] = jnp.where(fx[0], low, bx[u])
        my1[u] = jnp.where(fy[0], myu[u], myd[u])
        my2[u] = jnp.where(fy[0], myd[u], myu[u])
    mz[...] = fold(zm[...], 4 * nx)
    line = lax.broadcasted_iota(jnp.int32, (1, LANES), 1)
    row = jnp.zeros((1, LANES), jnp.float32)
    for k in range(accs.shape[0]):
        row = jnp.where(line == k, jnp.sum(accs[k]), row)
    sums[...] = jnp.broadcast_to(row, sums.shape)


def final_kernel(count, all_sums, v_ref, gp, hp, x1, x2, y1, y2, z1, z2, g_ref, h_ref, t_ref, halo):
    nx, ny, nz = v_ref.shape
    fx, fy, fz = edge_flags()
    row = jnp.sum(all_sums[...], axis=0, keepdims=True)
    line = lax.broadcasted_iota(jnp.int32, (1, LANES), 1)
    damping = jnp.sum(jnp.where(line == 9, row, 0.0)) * (0.5 / count)
    weight = jnp.where(line == 0, sh_zero, 0.0)
    for k, factor in enumerate((sh_one, sh_one, sh_one, sh_two, sh_two, 3.0 * sh_three, sh_two, sh_four)):
        weight = jnp.where(line == k + 1, factor, weight)
    shift = jnp.sum(jnp.where(line == 0, row, 0.0)) * sh_three
    t_ref[...] = (row * weight - jnp.where(line == 6, shift, 0.0))[0, :9]
    halo[...] = both_sides(fz, z1[...], z2[...], 4 * nx)
    lanes = lane_ids(ny)
    outer = (lanes == 0) | (lanes == LANES - 1)
    for u, (ref, out) in enumerate(((gp, g_ref), (hp, h_ref))):
        left, right = sides(fx, x1[u], x2[u])
        before, after = sides(fy, y1[u], y2[u])
        for x in range(nx):
            lane = u * nx + x
            value = ref[x + 1]
            value = value + jnp.where(outer, pltpu.roll(halo[...], LANES - 1 - 2 * lane, 1), 0.0)
            if u == 1:
                value = value + damping * v_ref[x]
            if x == 0:
                value = value + left
            if x == nx - 1:
                value = value + right
            out[x] = value
            out[x, 0:1, :] = out[x, 0:1, :] + before[x : x + 1]
            out[x, ny - 1 : ny, :] = out[x, ny - 1 : ny, :] + after[x : x + 1]


def exchange(firsts, seconds):
    got = []
    for axis, one, two in zip(AXES, firsts, seconds):
        count = lax.axis_size(axis)
        inner = [(i, i ^ 1) for i in range(count)]
        outer = [(i, ((((i + 1) % count) ^ 1) - 1) % count) for i in range(count)]
        got.append(lax.ppermute(one, axis, inner))
        got.append(lax.ppermute(two, axis, outer))
    return got


def body(sdf, albedo, intensity, direction, lighting):
    nx, ny, nz = sdf.shape
    devices = 1
    for axis in AXES:
        devices *= lax.axis_size(axis)
    count = float(nx * ny * nz) * devices
    f32 = lambda *shape: jax.ShapeDtypeStruct(shape, jnp.float32)
    rows = ny * 4 * nx // LANES
    faces = [f32(2, ny, nz)] * 2 + [f32(2, nx, nz)] * 2 + [f32(rows, LANES)]
    vmem = pl.BlockSpec(memory_space=pltpu.VMEM)
    smem = pl.BlockSpec(memory_space=pltpu.SMEM)
    scratch = lambda *shape: pltpu.VMEM(shape, jnp.float32)
    tall = ny + 2 * PAD

    x1, x2, y1, y2, zm = pl.pallas_call(
        pack_kernel,
        out_shape=faces,
        in_specs=[pl.BlockSpec(memory_space=pl.ANY)] * 2,
        out_specs=[vmem] * 5,
        scratch_shapes=[scratch(nx, ny, nz), scratch(nx, ny, nz), pltpu.SemaphoreType.DMA((2, 2))],
        compiler_params=PARAMS,
    )(sdf, direction)
    halos = exchange((x1, y1, zm), (x2, y2, zm))
    gp, hp, x1, x2, y1, y2, zm, sums = pl.pallas_call(
        main_kernel,
        out_shape=[f32(nx + 1, ny, nz)] * 2 + faces + [f32(devices, LANES)],
        in_specs=[smem] + [vmem] * 10,
        out_specs=[vmem] * 8,
        scratch_shapes=[
            scratch(nx + 2, tall, nz), scratch(nx + 2, tall, nz), scratch(ny, LANES),
            scratch(2, ny, nz), scratch(2, tall, nz), scratch(2, tall, nz), scratch(2, ny, nz),
            scratch(ny, LANES), scratch(2, nx, nz), scratch(2, nx, nz), scratch(10, ROWS, LANES),
        ],
        compiler_params=PARAMS,
    )(lighting, sdf, albedo, intensity, direction, *halos)
    halos = exchange((x1, y1, zm), (x2, y2, zm))
    all_sums = lax.all_to_all(sums, AXES, 0, 0, tiled=True)
    gradient, hess_vec, totals = pl.pallas_call(
        lambda *refs: final_kernel(count, *refs),
        out_shape=[f32(nx, ny, nz)] * 2 + [f32(9)],
        in_specs=[vmem] * 10,
        out_specs=[vmem] * 3,
        scratch_shapes=[scratch(ny, LANES)],
        compiler_params=PARAMS,
    )(all_sums, direction, gp, hp, *halos)
    return gradient, hess_vec, totals


def solution(mesh):
    grid = P("gx", "gy", "gz")
    return jax.shard_map(
        body,
        mesh=mesh,
        in_specs=(grid, grid, grid, grid, P()),
        out_specs=(grid, grid, P()),
        check_vma=False,
    )
```

```python
import jax
import jax.numpy as jnp
from jax import lax
from jax.experimental import pallas as pl
from jax.experimental.pallas import tpu as pltpu
from jax.sharding import PartitionSpec as P

reg_weight = 0.02
sh_zero = 0.282095
sh_one = 0.488603
sh_two = 1.092548
sh_three = 0.315392
sh_four = 0.546274

AXES = ("gx", "gy", "gz")
LANES = 128
ROWS = 8
PAD = 8
PARAMS = pltpu.CompilerParams(vmem_limit_bytes=40 * 1024 * 1024)


def lane_ids(rows):
    return lax.broadcasted_iota(jnp.int32, (rows, LANES), 1)


def fold(tall, width):
    parts = LANES // width
    rows = tall.shape[0] // parts
    lanes = lane_ids(rows)
    out = tall[:rows]
    for g in range(1, parts):
        moved = pltpu.roll(tall[g * rows : (g + 1) * rows], g * width, 1)
        out = jnp.where((lanes >= g * width) & (lanes < (g + 1) * width), moved, out)
    return out


def unfold(packed, width):
    parts = LANES // width
    pieces = [packed] + [pltpu.roll(packed, LANES - g * width, 1) for g in range(1, parts)]
    return jnp.concatenate(pieces, axis=0)


def edge_flags():
    flags = []
    for axis in AXES:
        index, count = lax.axis_index(axis), lax.axis_size(axis)
        flags.append(
            (
                lax.rem(index, 2) == 0,
                jnp.where(index > 0, 1.0, 0.0).astype(jnp.float32),
                jnp.where(index < count - 1, 1.0, 0.0).astype(jnp.float32),
            )
        )
    return flags


def sides(flag, first, second):
    even, before, after = flag
    return jnp.where(even, second, first) * before, jnp.where(even, first, second) * after


def both_sides(flag, first, second, width):
    before, after = sides(flag, first, second)
    odd = lax.rem(lane_ids(first.shape[0]), 2) == 1
    return unfold(jnp.where(odd, before, after), width)


def pack_kernel(d_hbm, v_hbm, x1, x2, y1, y2, zm, d_ref, v_ref, sems):
    nx, ny, nz = d_ref.shape
    half = nx // 2
    copies = []
    for f, (src, dst) in enumerate(((d_hbm, d_ref), (v_hbm, v_ref))):
        for h in range(2):
            part = pl.ds(h * half, half)
            copy = pltpu.make_async_copy(src.at[part], dst.at[part], sems.at[f, h])
            copy.start()
            copies.append(copy)
    (xe, _, _), (ye, _, _), _ = edge_flags()
    lanes = lane_ids(ny)
    edge = lanes == 0
    pair = lanes // 2
    packed = jnp.zeros((ny, LANES), jnp.float32)
    for f, ref in enumerate((d_ref, v_ref)):
        for h in range(2):
            copies[2 * f + h].wait()
            for x in range(h * half, (h + 1) * half):
                top, bottom = ref[x, ny - 1 : ny, :], ref[x, 0:1, :]
                y1[f, x : x + 1, :] = jnp.where(ye, top, bottom)
                y2[f, x : x + 1, :] = jnp.where(ye, bottom, top)
                plane = ref[x]
                slot = f * nx + x
                up = pltpu.roll(plane, (2 * slot + 2) % LANES, 1)
                down = pltpu.roll(plane, 2 * slot, 1) if slot else plane
                odd = lanes == 2 * slot + 1
                packed = jnp.where(odd, up, jnp.where(lanes == 2 * slot, down, packed))
        x1[f] = jnp.where(xe, ref[nx - 1], ref[0])
        x2[f] = jnp.where(xe, ref[0], ref[nx - 1])
    zm[...] = fold(packed, 4 * nx)


def main_kernel(
    light, d_ref, a_ref, i_ref, v_ref, x1, x2, y1, y2, z1, z2,
    gp, hp, mx1, mx2, my1, my2, mz, sums,
    dpad, vpad, halo, cent, ay, by, bx, zm, myu, myd, accs,
):
    nx, ny, nz = d_ref.shape
    fx, fy, fz = edge_flags()
    for f, (ref, pad) in enumerate(((d_ref, dpad), (v_ref, vpad))):
        pad[1 : nx + 1, PAD : PAD + ny, :] = ref[...]
        before, after = sides(fx, x1[f], x2[f])
        pad[0, PAD : PAD + ny, :] = before
        pad[nx + 1, PAD : PAD + ny, :] = after
        before, after = sides(fy, y1[f], y2[f])
        for x in range(nx):
            pad[x + 1, PAD - 1 : PAD, :] = before[x : x + 1]
            pad[x + 1, PAD + ny : PAD + ny + 1, :] = after[x : x + 1]
    halo[...] = both_sides(fz, z1[...], z2[...], 4 * nx)
    zero_row = jnp.zeros((1, LANES), jnp.float32)
    for u in range(2):
        ay[u, PAD + ny : PAD + ny + 1, :] = zero_row
        by[u, PAD - 1 : PAD, :] = zero_row
    zero = jnp.zeros((ROWS, LANES), jnp.float32)
    zm[...] = jnp.zeros((ny, LANES), jnp.float32)
    bx[...] = jnp.zeros(bx.shape, jnp.float32)
    gp[0] = jnp.zeros((ny, LANES), jnp.float32)
    hp[0] = jnp.zeros((ny, LANES), jnp.float32)
    for k in range(accs.shape[0]):
        accs[k] = zero

    l = [light[k] for k in range(9)]
    c1, c2, c3 = sh_one * l[1], sh_one * l[2], sh_one * l[3]
    c4, c5, c7 = sh_two * l[4], sh_two * l[5], sh_two * l[7]
    c6, c8 = 6.0 * sh_three * l[6], 2.0 * sh_four * l[8]
    base = sh_zero * l[0] - sh_three * l[6]
    lanes = lane_ids(ROWS)
    first, final, pair = lanes == 0, lanes == LANES - 1, lanes // 2

    def shifted(pad, f, x, at, mid):
        xm = pad[x, at : at + ROWS, :]
        xq = pad[x + 2, at : at + ROWS, :]
        ym = pad[x + 1, at - 1 : at - 1 + ROWS, :]
        yq = pad[x + 1, at + 1 : at + 1 + ROWS, :]
        lane = f * nx + x
        rows = slice(at - PAD, at - PAD + ROWS)
        edges = pltpu.roll(halo[rows, :], LANES - 1 - 2 * lane, 1)
        below = jnp.where(first, edges, pltpu.roll(mid, 1, 1))
        above = jnp.where(final, edges, pltpu.roll(mid, LANES - 1, 1))
        lap = (xm + xq) + (ym + yq) + (below + above) - 6.0 * mid
        return xq - xm, yq - ym, above - below, lap

    def plane(x, _):
        for c in range(ny // ROWS):
            at = PAD + c * ROWS
            rows = slice(c * ROWS, (c + 1) * ROWS)
            mid = dpad[x + 1, at : at + ROWS, :]
            hx, hy, hz, lap = shifted(dpad, 0, x, at, mid)
            inv = lax.rsqrt(hx * hx + hy * hy + hz * hz + 1.0)
            nrx, nry, nrz = hx * inv, hy * inv, hz * inv
            px = c3 + c4 * nry + c7 * nrz + c8 * nrx
            py = c1 + c4 * nrx + c5 * nrz - c8 * nry
            pz = c2 + c5 * nry + c7 * nrx + c6 * nrz
            along = nrx * px + nry * py + nrz * pz
            linear = c1 * nry + c2 * nrz + c3 * nrx
            shade = base + 0.5 * (along + linear)
            albedo = a_ref[x, rows, :]
            res = albedo * shade - i_ref[x, rows, :]
            qx, qy, qz = px - nrx * along, py - nry * along, pz - nrz * along
            scale = albedo * inv
            w = albedo * res
            wx, wy, wz = w * nrx, w * nry, w * nrz
            terms = (
                w, wy, wz, wx, wx * nry, wy * nrz, wz * nrz, wx * nrz,
                wx * nrx - wy * nry, res * res + reg_weight * (lap * lap),
            )
            for k, term in enumerate(terms):
                accs[k] = accs[k] + term
            vmid = vpad[x + 1, at : at + ROWS, :]
            ux, uy, uz, vlap = shifted(vpad, 1, x, at, vmid)
            lin = scale * (qx * ux + qy * uy + qz * uz)
            for u, (weight, lapl) in enumerate(((res * scale, lap), (lin * scale, vlap))):
                reg = reg_weight * lapl
                rx, ry, rz = weight * qx, weight * qy, weight * qz
                ay[u, at : at + ROWS, :] = reg - ry
                by[u, at : at + ROWS, :] = reg + ry
                lane = u * nx + x
                fwd = pltpu.roll(reg + rz, 1, 1)
                bwd = pltpu.roll(reg - rz, LANES - 1, 1)
                edges = pltpu.roll(jnp.where(first, fwd, bwd), 2 * lane + 1, 1)
                zm[rows, :] = jnp.where(pair == lane, edges, zm[rows, :])
                out = (gp, hp)[u]
                out[x, rows, :] = out[x, rows, :] + (reg - rx)
                cent[u, rows, :] = (
                    bx[u, rows, :]
                    - 6.0 * reg
                    + jnp.where(first, 0.0, fwd)
                    + jnp.where(final, 0.0, bwd)
                )
                bx[u, rows, :] = reg + rx
        for u in range(2):
            out = (gp, hp)[u]
            for c in range(ny // ROWS):
                at = PAD + c * ROWS
                rows = slice(c * ROWS, (c + 1) * ROWS)
                out[x + 1, rows, :] = (
                    cent[u, rows, :]
                    + ay[u, at + 1 : at + 1 + ROWS, :]
                    + by[u, at - 1 : at - 1 + ROWS, :]
                )
            myd[u, pl.ds(x, 1), :] = ay[u, PAD : PAD + 1, :]
            myu[u, pl.ds(x, 1), :] = by[u, PAD + ny - 1 : PAD + ny, :]
        return 0

    lax.fori_loop(0, nx, plane, 0, unroll=2)
    for u in range(2):
        low = (gp, hp)[u][0]
        mx1[u] = jnp.where(fx[0], bx[u], low)
        mx2[u] = jnp.where(fx[0], low, bx[u])
        my1[u] = jnp.where(fy[0], myu[u], myd[u])
        my2[u] = jnp.where(fy[0], myd[u], myu[u])
    mz[...] = fold(zm[...], 4 * nx)
    line = lax.broadcasted_iota(jnp.int32, (1, LANES), 1)
    row = jnp.zeros((1, LANES), jnp.float32)
    for k in range(accs.shape[0]):
        row = jnp.where(line == k, jnp.sum(accs[k]), row)
    sums[...] = jnp.broadcast_to(row, sums.shape)


def final_kernel(count, all_sums, v_ref, gp, hp, x1, x2, y1, y2, z1, z2, g_ref, h_ref, t_ref, halo):
    nx, ny, nz = v_ref.shape
    fx, fy, fz = edge_flags()
    row = jnp.sum(all_sums[...], axis=0, keepdims=True)
    line = lax.broadcasted_iota(jnp.int32, (1, LANES), 1)
    damping = jnp.sum(jnp.where(line == 9, row, 0.0)) * (0.5 / count)
    weight = jnp.where(line == 0, sh_zero, 0.0)
    for k, factor in enumerate((sh_one, sh_one, sh_one, sh_two, sh_two, 3.0 * sh_three, sh_two, sh_four)):
        weight = jnp.where(line == k + 1, factor, weight)
    shift = jnp.sum(jnp.where(line == 0, row, 0.0)) * sh_three
    t_ref[...] = (row * weight - jnp.where(line == 6, shift, 0.0))[0, :9]
    halo[...] = both_sides(fz, z1[...], z2[...], 4 * nx)
    lanes = lane_ids(ny)
    outer = (lanes == 0) | (lanes == LANES - 1)
    for u, (ref, out) in enumerate(((gp, g_ref), (hp, h_ref))):
        left, right = sides(fx, x1[u], x2[u])
        before, after = sides(fy, y1[u], y2[u])
        for x in range(nx):
            lane = u * nx + x
            value = ref[x + 1]
            value = value + jnp.where(outer, pltpu.roll(halo[...], LANES - 1 - 2 * lane, 1), 0.0)
            if u == 1:
                value = value + damping * v_ref[x]
            if x == 0:
                value = value + left
            if x == nx - 1:
                value = value + right
            out[x] = value
            out[x, 0:1, :] = out[x, 0:1, :] + before[x : x + 1]
            out[x, ny - 1 : ny, :] = out[x, ny - 1 : ny, :] + after[x : x + 1]


def exchange(firsts, seconds):
    got = []
    for axis, one, two in zip(AXES, firsts, seconds):
        count = lax.axis_size(axis)
        inner = [(i, i ^ 1) for i in range(count)]
        outer = [(i, ((((i + 1) % count) ^ 1) - 1) % count) for i in range(count)]
        got.append(lax.ppermute(one, axis, inner))
        got.append(lax.ppermute(two, axis, outer))
    return got


def body(sdf, albedo, intensity, direction, lighting):
    nx, ny, nz = sdf.shape
    devices = 1
    for axis in AXES:
        devices *= lax.axis_size(axis)
    count = float(nx * ny * nz) * devices
    f32 = lambda *shape: jax.ShapeDtypeStruct(shape, jnp.float32)
    rows = ny * 4 * nx // LANES
    faces = [f32(2, ny, nz)] * 2 + [f32(2, nx, nz)] * 2 + [f32(rows, LANES)]
    vmem = pl.BlockSpec(memory_space=pltpu.VMEM)
    smem = pl.BlockSpec(memory_space=pltpu.SMEM)
    scratch = lambda *shape: pltpu.VMEM(shape, jnp.float32)
    tall = ny + 2 * PAD

    x1, x2, y1, y2, zm = pl.pallas_call(
        pack_kernel,
        out_shape=faces,
        in_specs=[pl.BlockSpec(memory_space=pl.ANY)] * 2,
        out_specs=[vmem] * len(faces),
        scratch_shapes=[scratch(nx, ny, nz), scratch(nx, ny, nz), pltpu.SemaphoreType.DMA((2, 2))],
        compiler_params=PARAMS,
    )(sdf, direction)
    halos = exchange((x1, y1, zm), (x2, y2, zm))
    gp, hp, x1, x2, y1, y2, zm, sums = pl.pallas_call(
        main_kernel,
        out_shape=[f32(nx + 1, ny, nz)] * 2 + faces + [f32(devices, LANES)],
        in_specs=[smem] + [vmem] * 10,
        out_specs=[vmem] * (len(faces) + 3),
        scratch_shapes=[
            scratch(nx + 2, tall, nz), scratch(nx + 2, tall, nz), scratch(ny, LANES),
            scratch(2, ny, nz), scratch(2, tall, nz), scratch(2, tall, nz), scratch(2, ny, nz),
            scratch(ny, LANES), scratch(2, nx, nz), scratch(2, nx, nz), scratch(10, ROWS, LANES),
        ],
        compiler_params=PARAMS,
    )(lighting, sdf, albedo, intensity, direction, *halos)
    halos = exchange((x1, y1, zm), (x2, y2, zm))
    all_sums = lax.all_to_all(sums, AXES, 0, 0, tiled=True)
    gradient, hess_vec, totals = pl.pallas_call(
        lambda *refs: final_kernel(count, *refs),
        out_shape=[f32(nx, ny, nz)] * 2 + [f32(9)],
        in_specs=[vmem] * 10,
        out_specs=[vmem] * 3,
        scratch_shapes=[scratch(ny, LANES)],
        compiler_params=PARAMS,
    )(all_sums, direction, gp, hp, *halos)
    return gradient, hess_vec, totals


def solution(mesh):
    grid = P("gx", "gy", "gz")
    return jax.shard_map(
        body,
        mesh=mesh,
        in_specs=(grid, grid, grid, grid, P()),
        out_specs=(grid, grid, P()),
        check_vma=False,
    )
```

```python
import jax
import jax.numpy as jnp
from jax import lax
from jax.experimental import pallas as pl
from jax.experimental.pallas import tpu as pltpu
from jax.sharding import PartitionSpec as P

reg_weight = 0.02
sh_zero = 0.282095
sh_one = 0.488603
sh_two = 1.092548
sh_three = 0.315392
sh_four = 0.546274

AXES = ("gx", "gy", "gz")
LANES = 128
ROWS = 8
PAD = 8
PARAMS = pltpu.CompilerParams(vmem_limit_bytes=40 * 1024 * 1024)
FULL = pltpu.CompilerParams(vmem_limit_bytes=62 * 1024 * 1024)


def lane_ids(rows):
    return lax.broadcasted_iota(jnp.int32, (rows, LANES), 1)


def fold(tall, width):
    parts = LANES // width
    rows = tall.shape[0] // parts
    lanes = lane_ids(rows)
    out = tall[:rows]
    for g in range(1, parts):
        moved = pltpu.roll(tall[g * rows : (g + 1) * rows], g * width, 1)
        out = jnp.where((lanes >= g * width) & (lanes < (g + 1) * width), moved, out)
    return out


def unfold(packed, width):
    parts = LANES // width
    pieces = [packed] + [pltpu.roll(packed, LANES - g * width, 1) for g in range(1, parts)]
    return jnp.concatenate(pieces, axis=0)


def edge_flags():
    flags = []
    for axis in AXES:
        index, count = lax.axis_index(axis), lax.axis_size(axis)
        flags.append(
            (
                lax.rem(index, 2) == 0,
                jnp.where(index > 0, 1.0, 0.0).astype(jnp.float32),
                jnp.where(index < count - 1, 1.0, 0.0).astype(jnp.float32),
            )
        )
    return flags


def sides(flag, first, second):
    even, before, after = flag
    return jnp.where(even, second, first) * before, jnp.where(even, first, second) * after


def both_sides(flag, first, second, width):
    before, after = sides(flag, first, second)
    odd = lax.rem(lane_ids(first.shape[0]), 2) == 1
    return unfold(jnp.where(odd, before, after), width)


def pack_x_kernel(d_hbm, v_hbm, x1, x2, sems):
    nx = d_hbm.shape[0]
    (even, _, _), _, _ = edge_flags()
    one = jnp.where(even, nx - 1, 0)
    copies = []
    for f, src in enumerate((d_hbm, v_hbm)):
        copies.append(pltpu.make_async_copy(src.at[one], x1.at[f], sems.at[f, 0]))
        copies.append(pltpu.make_async_copy(src.at[nx - 1 - one], x2.at[f], sems.at[f, 1]))
    for copy in copies:
        copy.start()
    for copy in copies:
        copy.wait()


def pack_yz_kernel(d_ref, v_ref, y1, y2, zm):
    nx, ny, nz = d_ref.shape
    _, (even, _, _), _ = edge_flags()
    lanes = lane_ids(ny)
    packed = jnp.zeros((ny, LANES), jnp.float32)
    for f, ref in enumerate((d_ref, v_ref)):
        for x in range(nx):
            top, bottom = ref[x, ny - 1 : ny, :], ref[x, 0:1, :]
            y1[f, x : x + 1, :] = jnp.where(even, top, bottom)
            y2[f, x : x + 1, :] = jnp.where(even, bottom, top)
            plane = ref[x]
            slot = f * nx + x
            up = pltpu.roll(plane, (2 * slot + 2) % LANES, 1)
            down = pltpu.roll(plane, 2 * slot, 1) if slot else plane
            odd = lanes == 2 * slot + 1
            packed = jnp.where(odd, up, jnp.where(lanes == 2 * slot, down, packed))
    zm[...] = fold(packed, 4 * nx)


def main_kernel(
    light, d_ref, a_ref, i_ref, v_ref, x1, x2, y1, y2, z1, z2,
    gp, hp, mx1, mx2, my1, my2, mz, sums,
    dpad, vpad, halo, cent, ay, by, bx, zm, myu, myd, accs,
):
    nx, ny, nz = d_ref.shape
    fx, fy, fz = edge_flags()
    for f, (ref, pad) in enumerate(((d_ref, dpad), (v_ref, vpad))):
        pad[1 : nx + 1, PAD : PAD + ny, :] = ref[...]
        before, after = sides(fx, x1[f], x2[f])
        pad[0, PAD : PAD + ny, :] = before
        pad[nx + 1, PAD : PAD + ny, :] = after
        before, after = sides(fy, y1[f], y2[f])
        for x in range(nx):
            pad[x + 1, PAD - 1 : PAD, :] = before[x : x + 1]
            pad[x + 1, PAD + ny : PAD + ny + 1, :] = after[x : x + 1]
    halo[...] = both_sides(fz, z1[...], z2[...], 4 * nx)
    zero_row = jnp.zeros((1, LANES), jnp.float32)
    for u in range(2):
        ay[u, PAD + ny : PAD + ny + 1, :] = zero_row
        by[u, PAD - 1 : PAD, :] = zero_row
    zero = jnp.zeros((ROWS, LANES), jnp.float32)
    zm[...] = jnp.zeros((ny, LANES), jnp.float32)
    bx[...] = jnp.zeros(bx.shape, jnp.float32)
    gp[0] = jnp.zeros((ny, LANES), jnp.float32)
    hp[0] = jnp.zeros((ny, LANES), jnp.float32)
    for k in range(accs.shape[0]):
        accs[k] = zero

    l = [light[k] for k in range(9)]
    c1, c2, c3 = sh_one * l[1], sh_one * l[2], sh_one * l[3]
    c4, c5, c7 = sh_two * l[4], sh_two * l[5], sh_two * l[7]
    c6, c8 = 6.0 * sh_three * l[6], 2.0 * sh_four * l[8]
    base = sh_zero * l[0] - sh_three * l[6]
    lanes = lane_ids(ROWS)
    first, final, pair = lanes == 0, lanes == LANES - 1, lanes // 2

    def shifted(pad, f, x, at, mid):
        xm = pad[x, at : at + ROWS, :]
        xq = pad[x + 2, at : at + ROWS, :]
        ym = pad[x + 1, at - 1 : at - 1 + ROWS, :]
        yq = pad[x + 1, at + 1 : at + 1 + ROWS, :]
        lane = f * nx + x
        rows = slice(at - PAD, at - PAD + ROWS)
        edges = pltpu.roll(halo[rows, :], LANES - 1 - 2 * lane, 1)
        below = jnp.where(first, edges, pltpu.roll(mid, 1, 1))
        above = jnp.where(final, edges, pltpu.roll(mid, LANES - 1, 1))
        lap = (xm + xq) + (ym + yq) + (below + above) - 6.0 * mid
        return xq - xm, yq - ym, above - below, lap

    def plane(x, _):
        for c in range(ny // ROWS):
            at = PAD + c * ROWS
            rows = slice(c * ROWS, (c + 1) * ROWS)
            mid = dpad[x + 1, at : at + ROWS, :]
            hx, hy, hz, lap = shifted(dpad, 0, x, at, mid)
            inv = lax.rsqrt(hx * hx + hy * hy + hz * hz + 1.0)
            nrx, nry, nrz = hx * inv, hy * inv, hz * inv
            px = c3 + c4 * nry + c7 * nrz + c8 * nrx
            py = c1 + c4 * nrx + c5 * nrz - c8 * nry
            pz = c2 + c5 * nry + c7 * nrx + c6 * nrz
            along = nrx * px + nry * py + nrz * pz
            linear = c1 * nry + c2 * nrz + c3 * nrx
            shade = base + 0.5 * (along + linear)
            albedo = a_ref[x, rows, :]
            res = albedo * shade - i_ref[x, rows, :]
            qx, qy, qz = px - nrx * along, py - nry * along, pz - nrz * along
            scale = albedo * inv
            w = albedo * res
            wx, wy, wz = w * nrx, w * nry, w * nrz
            terms = (
                w, wy, wz, wx, wx * nry, wy * nrz, wz * nrz, wx * nrz,
                wx * nrx - wy * nry, res * res + reg_weight * (lap * lap),
            )
            for k, term in enumerate(terms):
                accs[k] = accs[k] + term
            vmid = vpad[x + 1, at : at + ROWS, :]
            ux, uy, uz, vlap = shifted(vpad, 1, x, at, vmid)
            lin = scale * (qx * ux + qy * uy + qz * uz)
            for u, (weight, lapl) in enumerate(((res * scale, lap), (lin * scale, vlap))):
                reg = reg_weight * lapl
                rx, ry, rz = weight * qx, weight * qy, weight * qz
                ay[u, at : at + ROWS, :] = reg - ry
                by[u, at : at + ROWS, :] = reg + ry
                lane = u * nx + x
                fwd = pltpu.roll(reg + rz, 1, 1)
                bwd = pltpu.roll(reg - rz, LANES - 1, 1)
                edges = pltpu.roll(jnp.where(first, fwd, bwd), 2 * lane + 1, 1)
                zm[rows, :] = jnp.where(pair == lane, edges, zm[rows, :])
                out = (gp, hp)[u]
                out[x, rows, :] = out[x, rows, :] + (reg - rx)
                cent[u, rows, :] = (
                    bx[u, rows, :]
                    - 6.0 * reg
                    + jnp.where(first, 0.0, fwd)
                    + jnp.where(final, 0.0, bwd)
                )
                bx[u, rows, :] = reg + rx
        for u in range(2):
            out = (gp, hp)[u]
            for c in range(ny // ROWS):
                at = PAD + c * ROWS
                rows = slice(c * ROWS, (c + 1) * ROWS)
                out[x + 1, rows, :] = (
                    cent[u, rows, :]
                    + ay[u, at + 1 : at + 1 + ROWS, :]
                    + by[u, at - 1 : at - 1 + ROWS, :]
                )
            myd[u, pl.ds(x, 1), :] = ay[u, PAD : PAD + 1, :]
            myu[u, pl.ds(x, 1), :] = by[u, PAD + ny - 1 : PAD + ny, :]
        return 0

    lax.fori_loop(0, nx, plane, 0, unroll=2)
    for u in range(2):
        low = (gp, hp)[u][0]
        mx1[u] = jnp.where(fx[0], bx[u], low)
        mx2[u] = jnp.where(fx[0], low, bx[u])
        my1[u] = jnp.where(fy[0], myu[u], myd[u])
        my2[u] = jnp.where(fy[0], myd[u], myu[u])
    mz[...] = fold(zm[...], 4 * nx)
    line = lax.broadcasted_iota(jnp.int32, (1, LANES), 1)
    row = jnp.zeros((1, LANES), jnp.float32)
    for k in range(accs.shape[0]):
        row = jnp.where(line == k, jnp.sum(accs[k]), row)
    sums[...] = jnp.broadcast_to(row, sums.shape)


def final_kernel(count, all_sums, v_ref, gp, hp, x1, x2, y1, y2, z1, z2, g_ref, h_ref, t_ref, halo):
    nx, ny, nz = v_ref.shape
    fx, fy, fz = edge_flags()
    row = jnp.sum(all_sums[...], axis=0, keepdims=True)
    line = lax.broadcasted_iota(jnp.int32, (1, LANES), 1)
    damping = jnp.sum(jnp.where(line == 9, row, 0.0)) * (0.5 / count)
    weight = jnp.where(line == 0, sh_zero, 0.0)
    for k, factor in enumerate((sh_one, sh_one, sh_one, sh_two, sh_two, 3.0 * sh_three, sh_two, sh_four)):
        weight = jnp.where(line == k + 1, factor, weight)
    shift = jnp.sum(jnp.where(line == 0, row, 0.0)) * sh_three
    t_ref[...] = (row * weight - jnp.where(line == 6, shift, 0.0))[0, :9]
    halo[...] = both_sides(fz, z1[...], z2[...], 4 * nx)
    lanes = lane_ids(ny)
    outer = (lanes == 0) | (lanes == LANES - 1)
    for u, (ref, out) in enumerate(((gp, g_ref), (hp, h_ref))):
        left, right = sides(fx, x1[u], x2[u])
        before, after = sides(fy, y1[u], y2[u])
        for x in range(nx):
            lane = u * nx + x
            value = ref[x + 1]
            value = value + jnp.where(outer, pltpu.roll(halo[...], LANES - 1 - 2 * lane, 1), 0.0)
            if u == 1:
                value = value + damping * v_ref[x]
            if x == 0:
                value = value + left
            if x == nx - 1:
                value = value + right
            out[x] = value
            out[x, 0:1, :] = out[x, 0:1, :] + before[x : x + 1]
            out[x, ny - 1 : ny, :] = out[x, ny - 1 : ny, :] + after[x : x + 1]


def exchange(firsts, seconds):
    got = []
    for axis, one, two in zip(AXES, firsts, seconds):
        count = lax.axis_size(axis)
        inner = [(i, i ^ 1) for i in range(count)]
        outer = [(i, ((((i + 1) % count) ^ 1) - 1) % count) for i in range(count)]
        got.append(lax.ppermute(one, axis, inner))
        got.append(lax.ppermute(two, axis, outer))
    return got


def body(sdf, albedo, intensity, direction, lighting):
    nx, ny, nz = sdf.shape
    devices = 1
    for axis in AXES:
        devices *= lax.axis_size(axis)
    count = float(nx * ny * nz) * devices
    f32 = lambda *shape: jax.ShapeDtypeStruct(shape, jnp.float32)
    rows = ny * 4 * nx // LANES
    faces = [f32(2, ny, nz)] * 2 + [f32(2, nx, nz)] * 2 + [f32(rows, LANES)]
    vmem = pl.BlockSpec(memory_space=pltpu.VMEM)
    smem = pl.BlockSpec(memory_space=pltpu.SMEM)
    scratch = lambda *shape: pltpu.VMEM(shape, jnp.float32)
    tall = ny + 2 * PAD

    x1, x2 = pl.pallas_call(
        pack_x_kernel,
        out_shape=faces[:2],
        in_specs=[pl.BlockSpec(memory_space=pl.ANY)] * 2,
        out_specs=[vmem] * 2,
        scratch_shapes=[pltpu.SemaphoreType.DMA((2, 2))],
        compiler_params=FULL,
    )(sdf, direction)
    y1, y2, zm = pl.pallas_call(
        pack_yz_kernel, out_shape=faces[2:], in_specs=[vmem] * 2, out_specs=[vmem] * 3, compiler_params=PARAMS
    )(sdf, direction)
    halos = exchange((x1, y1, zm), (x2, y2, zm))
    gp, hp, x1, x2, y1, y2, zm, sums = pl.pallas_call(
        main_kernel,
        out_shape=[f32(nx + 1, ny, nz)] * 2 + faces + [f32(devices, LANES)],
        in_specs=[smem] + [vmem] * 10,
        out_specs=[vmem] * (len(faces) + 3),
        scratch_shapes=[
            scratch(nx + 2, tall, nz), scratch(nx + 2, tall, nz), scratch(ny, LANES),
            scratch(2, ny, nz), scratch(2, tall, nz), scratch(2, tall, nz), scratch(2, ny, nz),
            scratch(ny, LANES), scratch(2, nx, nz), scratch(2, nx, nz), scratch(10, ROWS, LANES),
        ],
        compiler_params=PARAMS,
    )(lighting, sdf, albedo, intensity, direction, *halos)
    halos = exchange((x1, y1, zm), (x2, y2, zm))
    all_sums = lax.all_to_all(sums, AXES, 0, 0, tiled=True)
    gradient, hess_vec, totals = pl.pallas_call(
        lambda *refs: final_kernel(count, *refs),
        out_shape=[f32(nx, ny, nz)] * 2 + [f32(9)],
        in_specs=[vmem] * 10,
        out_specs=[vmem] * 3,
        scratch_shapes=[scratch(ny, LANES)],
        compiler_params=PARAMS,
    )(all_sums, direction, gp, hp, *halos)
    return gradient, hess_vec, totals


def solution(mesh):
    grid = P("gx", "gy", "gz")
    return jax.shard_map(
        body,
        mesh=mesh,
        in_specs=(grid, grid, grid, grid, P()),
        out_specs=(grid, grid, P()),
        check_vma=False,
    )
```
